1024 devices in a mesh: docs: 128 (over z, x, y_lo), terms: 8 (over y_hi, core).
Axes of the slice: x: 4, y: 8 (y_hi: 4, y_lo: 2; y = y_hi * 2 + y_lo), z: 16, core: 2. Of those that a mesh axis runs over, the one named last changes fastest.
Arguments:
- tile_values: bfloat16 [49152, 128, 128], P(('docs', 'terms')), may hold values from 0 to 0.03125
- tile_rows: int32 [49152], P(('docs', 'terms')), may hold values from 0 to 767, as said below
- tile_cols: int32 [49152], P(('docs', 'terms')), may hold values from 0 to 4095, as said below
- tile_count: int32 [1024], P(('docs', 'terms')), may hold values from 16 to 48, as said below
- labels: int32 [98304], P('docs'), may hold values from 0 to 127
- operands: bfloat16 [524288, 512], P(('docs', 'terms')), may hold values from -18 to 46
Outputs:
- newton_terms: float32 [524288, 512], P(('docs', 'terms'))
The draws below stay inside these ranges and needn't reach their ends.
Inputs may be any that keep to these rules, and one draw needn't show every extreme that they name: `tile_rows`: write the group of slot i as g = i // 48 = a * 8 + b. Its row block lies in a * 6 to (a + 1) * 6 - 1. `tile_cols`: with a and b as for tile_rows, the column block c of slot i has (c // 4) % 8 == b, and c // 32 is a - 1, a or a + 1 modulo 128. No two slots of a group name the same pair of row and column blocks. `tile_count`: some group has all 48 slots live.
All inputs are finite; a program needn't handle non-finite values.
Results may differ from the reference program's by a relative error of at most 0.0003.
Values may be sent and summed in bfloat16 or wider, within the bound.
No kernel may reach another device: no remote copies, remote signals or barrier semaphores. Data moves between devices by JAX's collectives and lax.ppermute only.
A program may use at most 32 MiB of HBM per device.

```python
import jax
import jax.numpy as jnp
from jax import lax

K = 128
BLOCK = 128
CB_DEV = 4
RB_DEV = 6
TILE_DEV = 48
TILES = 49152
ROWS = 98304
FEATS = 524288
N_DOCS = 128
N_TERMS = 8
DEVICES = 1024


def tile_slots(key):
    group_keys = jax.random.split(key, DEVICES)
    slot_total = RB_DEV * 3 * CB_DEV
    picks = jax.vmap(lambda group_key: jax.random.permutation(group_key, slot_total)[:TILE_DEV])(group_keys)
    return picks.astype(jnp.int32)


def draw_tile_rows(key, part):
    picks = tile_slots(key)
    group_ids = jnp.arange(DEVICES, dtype=jnp.int32)[:, None]
    docs_pos = group_ids // N_TERMS
    rows_out = docs_pos * RB_DEV + picks // (3 * CB_DEV)
    return rows_out.reshape(DEVICES * TILE_DEV).astype(jnp.int32)


def draw_tile_cols(key, part):
    picks = tile_slots(key)
    group_ids = jnp.arange(DEVICES, dtype=jnp.int32)[:, None]
    docs_pos = group_ids // N_TERMS
    term_pos = group_ids % N_TERMS
    remain = picks % (3 * CB_DEV)
    band = remain // CB_DEV
    within = remain % CB_DEV
    owner_pos = (docs_pos + band - 1 + N_DOCS) % N_DOCS
    cols_out = (owner_pos * N_TERMS + term_pos) * CB_DEV + within
    return cols_out.reshape(DEVICES * TILE_DEV).astype(jnp.int32)


def draw_tile_count(key, part):
    key = jax.random.fold_in(key, 5)
    first_key, second_key = jax.random.split(key)
    counts = jax.random.randint(first_key, (DEVICES,), max(TILE_DEV // 3, 1), TILE_DEV + 1, dtype=jnp.int32)
    fullest = jax.random.randint(second_key, (), 0, DEVICES, dtype=jnp.int32)
    return counts.at[fullest].set(TILE_DEV)


def draw_operands(key, part):
    key = jax.random.fold_in(key, 7)
    first_key = jax.random.fold_in(key, 0)
    third_key = jax.random.fold_in(key, 2)
    depth = jax.random.uniform(third_key, (K,), jnp.float32, 0.0, 1.0)
    weight_shift = -0.12 * depth
    direction_shift = 20.0 * jnp.exp(10.0 * (depth - 1.0))
    shift = jnp.concatenate([weight_shift, direction_shift, direction_shift, direction_shift])
    column = jnp.arange(4 * K, dtype=jnp.int32)
    noise = jnp.clip(jax.random.normal(first_key, (FEATS, 4 * K), jnp.float32), -6.0, 6.0)
    spread = jnp.where(column < K, 0.6, 3.0).astype(jnp.float32)
    values = noise * spread[None, :] + shift[None, :]
    return values.astype(jnp.bfloat16)


def touch_ends(entries, stream_key, low, high):
    shape = entries.shape
    place = [jax.random.randint(jax.random.fold_in(stream_key, axis), (), 0, shape[axis]) for axis in range(len(shape))]
    entries = entries.at[tuple(place)].set(low)
    longest = shape.index(max(shape))
    place[longest] = (place[longest] + 1) % shape[longest]
    return entries.at[tuple(place)].set(high)


def block_levels(stream_key, extent, cuts, least, high):
    factor_of = 1.0
    for position, shards_of in cuts:
        draws = jax.random.uniform(jax.random.fold_in(jax.random.fold_in(stream_key, 6), position), (shards_of,), jnp.float32, least / len(cuts), high / len(cuts))
        factor_of = factor_of * jnp.repeat(jnp.exp(draws), extent[position] // shards_of).reshape((-1,) + (1,) * (len(extent) - 1 - position))
    return factor_of


def setup_inputs(seed: int = 0) -> dict:
    splits = jax.random.split(jax.random.key(seed), 7)
    return {
        "tile_values": jnp.clip(0.03125 * jax.random.uniform(splits[0], (TILES, BLOCK, BLOCK), jnp.float32) ** block_levels(splits[0], (TILES, BLOCK, BLOCK), ((0, 1024),), -0.2, 0.2), 0.0, 0.03125).astype(jnp.bfloat16),
        "tile_rows": draw_tile_rows(jax.random.fold_in(splits[6], 71), 0),
        "tile_cols": draw_tile_cols(jax.random.fold_in(splits[6], 71), 0),
        "tile_count": draw_tile_count(jax.random.fold_in(splits[6], 71), 0),
        "labels": touch_ends(jax.random.randint(splits[4], (ROWS,), 0, K), jax.random.fold_in(splits[4], 1), 0, K - 1).astype(jnp.int32),
        "operands": draw_operands(jax.random.fold_in(splits[6], 71), 0),
    }


loss_weight = 4.0


def residual_rows(combined, labels):
    classes = combined.shape[1] // 4
    row_count = combined.shape[0]
    logits = combined[:, :classes]
    largest = jnp.max(logits, axis=1, keepdims=True)
    shifted = jnp.exp(logits - largest)
    probability = shifted / jnp.sum(shifted, axis=1, keepdims=True)
    onehot = (labels[:, None] == jnp.arange(classes, dtype=jnp.int32)[None, :]).astype(probability.dtype)
    images = combined[:, classes:].reshape(row_count, 3, classes)
    weighted = probability[:, None, :] * images
    curvature = weighted - probability[:, None, :] * jnp.sum(weighted, axis=2, keepdims=True)
    stacked = jnp.concatenate([(probability - onehot)[:, None, :], curvature], axis=1)
    return stacked.reshape(row_count, 4 * classes).astype(jnp.bfloat16)


def reference(tile_values, tile_rows, tile_cols, tile_count, labels, operands):
    stack_width = 4 * K
    tile_live = (jnp.arange(TILES, dtype=jnp.int32) % TILE_DEV) < jnp.repeat(tile_count, TILE_DEV)
    masked = jnp.where(tile_live[:, None, None], tile_values, jnp.zeros_like(tile_values))
    group_tiles = masked.reshape(DEVICES, TILE_DEV, BLOCK, BLOCK)
    group_rows = tile_rows.reshape(DEVICES, TILE_DEV)
    group_cols = tile_cols.reshape(DEVICES, TILE_DEV)
    col_blocks = operands.reshape(FEATS // BLOCK, BLOCK, stack_width)

    def forward(carry, scanned):
        tile_set, row_ids, col_ids = scanned
        blocks = jnp.take(col_blocks, col_ids, axis=0).astype(jnp.float32)
        products = jnp.einsum('tij,tjk->tik', tile_set.astype(jnp.float32), blocks)
        return carry.at[row_ids].add(products), None

    start_rows = jnp.zeros((ROWS // BLOCK, BLOCK, stack_width), jnp.float32)
    combined, _ = lax.scan(forward, start_rows, (group_tiles, group_rows, group_cols))
    residual = residual_rows(combined.reshape(ROWS, stack_width), labels)
    res_blocks = residual.reshape(ROWS // BLOCK, BLOCK, stack_width)

    def backward(carry, scanned):
        tile_set, row_ids, col_ids = scanned
        picked = jnp.take(res_blocks, row_ids, axis=0).astype(jnp.float32)
        products = jnp.einsum('tji,tjk->tik', tile_set.astype(jnp.float32), picked)
        return carry.at[col_ids].add(products), None

    start_cols = jnp.zeros((FEATS // BLOCK, BLOCK, stack_width), jnp.float32)
    transposed, _ = lax.scan(backward, start_cols, (group_tiles, group_rows, group_cols))
    return loss_weight * transposed.reshape(FEATS, stack_width)
```

```python
import functools

import jax
import jax.numpy as jnp
from jax import lax
from jax.experimental import pallas as pl
from jax.experimental.pallas import tpu as pltpu
from jax.sharding import PartitionSpec as P

loss_weight = 4.0
F32 = jnp.float32
BF16 = jnp.bfloat16
VMEM = pl.BlockSpec(memory_space=pltpu.VMEM)
SMEM = pl.BlockSpec(memory_space=pltpu.SMEM)

FORWARD_CUTS = ((0, 256), (256, 512))

SPAN = 205.0
LOWEST = 2.0**-3.75
SCALE_ROWS = 16
SMALLEST = 1e-30


def call(kernel, outs, *args, specs=None, flops=0, scratch=()):
    size = sum(o.size * o.dtype.itemsize for o in outs) + sum(a.size * a.dtype.itemsize for a in args)
    return pl.pallas_call(
        kernel,
        out_shape=outs,
        in_specs=specs or [VMEM] * len(args),
        out_specs=[VMEM] * len(outs),
        scratch_shapes=scratch,
        cost_estimate=pl.CostEstimate(flops=flops, bytes_accessed=size, transcendentals=0),
        compiler_params=pltpu.CompilerParams(vmem_limit_bytes=32 * 2**20),
    )(*args)


def shape(dims, dtype):
    return jax.ShapeDtypeStruct(dims, dtype)


def slab_kernel(docs_count, terms_count, place, rows, cols, count, tiles, slab, turned, starts):
    slots, block = tiles.shape[0], tiles.shape[1]
    docs_index, core, chip = place[0], place[1], place[2]
    height, width = slab.shape
    chunk = height // terms_count
    chips = terms_count // 2
    piece = block // 4
    row_blocks = height // block
    col_blocks = width // (3 * block)
    for part in range(height // piece):
        owner, inside = divmod(part, chunk // piece)
        half, owner_chip = divmod(owner, chips)
        mine = jnp.where(core == half, chips, 0)
        slot = mine + lax.rem(owner_chip - chip + chips, chips)
        starts[part] = slot * chunk + inside * piece
    slab[...] = jnp.zeros_like(slab)

    def put(tile, carry):
        col = cols[tile]
        band = lax.rem(lax.div(col, terms_count * col_blocks) - docs_index + 1 + docs_count, docs_count)
        lane = pl.multiple_of((band * col_blocks + lax.rem(col, col_blocks)) * block, block)
        row = rows[tile] - docs_index * row_blocks
        for part in range(4):
            to = pl.multiple_of(starts[row * 4 + part], piece)
            slab[pl.ds(to, piece), pl.ds(lane, block)] = tiles[tile, part * piece : (part + 1) * piece, :]
        return carry

    lax.fori_loop(0, jnp.minimum(count[0], slots), put, 0)
    for col in range(0, width, block):
        turned[col : col + block, :] = slab[:, col : col + block].T


def forward_kernel(slab, left, own, right, away, kept):
    depth = own.shape[0]
    half = slab.shape[0] // 2
    for out, top in ((away, 0), (kept, half)):
        total = jnp.dot(slab[top : top + half, :depth], left[...], preferred_element_type=F32)
        total += jnp.dot(slab[top : top + half, depth : 2 * depth], own[...], preferred_element_type=F32)
        total += jnp.dot(slab[top : top + half, 2 * depth :], right[...], preferred_element_type=F32)
        out[...] = total


def share_kernel(kept, come, *outs):
    chunk = outs[0].shape[0]
    for i, out in enumerate(outs):
        part = slice(i * chunk, (i + 1) * chunk)
        out[...] = kept[part, :] + come[part, :]


def residual_kernel(labels, *refs):
    parts, out = refs[:-1], refs[-1]
    combined = []
    for own, behind, ahead, across in zip(*[iter(parts)] * 4):
        combined.append((own[...] + behind[...]) + (ahead[...] + across[...]))
    combined = jnp.concatenate(combined, axis=1)
    classes = combined.shape[1] // 4
    logits = combined[:, :classes]
    shifted = jnp.exp(logits - jnp.max(logits, axis=1, keepdims=True))
    probability = shifted / jnp.sum(shifted, axis=1, keepdims=True)
    onehot = (lax.broadcasted_iota(jnp.int32, logits.shape, 1) == labels[...]).astype(F32)
    out[:, :classes] = (probability - onehot).astype(BF16)
    for j in range(1, 4):
        weighted = probability * combined[:, j * classes : (j + 1) * classes]
        curvature = weighted - probability * jnp.sum(weighted, axis=1, keepdims=True)
        out[:, j * classes : (j + 1) * classes] = curvature.astype(BF16)


def encode(values, out):
    rows = values.shape[0]
    scale = jnp.max(jnp.abs(values), axis=0, keepdims=True)
    scale = jnp.maximum(scale, SMALLEST).astype(BF16)
    out[rows:, :] = jnp.broadcast_to(scale, (SCALE_ROWS, scale.shape[1]))
    ratio = (SPAN * LOWEST) / scale.astype(F32)
    code = LOWEST + jnp.abs(values) * ratio
    for _ in range(5):
        code = code * code
    out[:rows, :] = jnp.where(values < 0, -code, code).astype(BF16)


def decode(code, scale):
    size = jnp.exp2(jnp.log2(jnp.abs(code)) * 0.03125 + 3.75) - 1.0
    size = size * (scale * (1.0 / SPAN))
    return jnp.where(code < 0, -size, size)


def send_kernel(turned, far, near, to_left, to_right):
    depth = turned.shape[0] // 3
    half = turned.shape[1] // 2
    for out, top in ((to_left, 0), (to_right, 2 * depth)):
        total = jnp.dot(turned[top : top + depth, :half], far[...], preferred_element_type=F32)
        total += jnp.dot(turned[top : top + depth, half:], near[...], preferred_element_type=F32)
        encode(total, out)


def own_kernel(turned, far, near, out):
    depth = turned.shape[0] // 3
    half = turned.shape[1] // 2
    total = jnp.dot(turned[depth : 2 * depth, :half], far[...], preferred_element_type=F32)
    total += jnp.dot(turned[depth : 2 * depth, half:], near[...], preferred_element_type=F32)
    out[...] = total


def total_kernel(own, one, two, out):
    rows = own.shape[0]
    step = 128

    def add(i, carry):
        part = pl.ds(pl.multiple_of(i * step, step), step)
        total = own[part, :]
        for code in (one, two):
            scale = code[rows : rows + SCALE_ROWS, :].astype(F32)[0:1, :]
            total += decode(code[part, :].astype(F32), scale)
        out[part, :] = loss_weight * total
        return carry

    lax.fori_loop(0, rows // step, add, 0)


def shifted(value, axis, by):
    size = lax.axis_size(axis)
    return lax.ppermute(value, axis, [(i, (i + by) % size) for i in range(size)])


def to_chip(value, by):
    size = lax.axis_size("terms")
    return lax.ppermute(value, "terms", [(i, (i + 2 * by) % size) for i in range(size)])


def to_core(value):
    size = lax.axis_size("terms")
    return lax.ppermute(value, "terms", [(i, i ^ 1) for i in range(size)])


def on_device(tile_values, tile_rows, tile_cols, tile_count, labels, operands):
    docs_count = lax.axis_size("docs")
    terms_count = lax.axis_size("terms")
    docs_index = lax.axis_index("docs")
    terms_index = lax.axis_index("terms")
    core, chip = terms_index % 2, terms_index // 2
    block = tile_values.shape[1]
    depth, classes4 = operands.shape
    height = labels.shape[0]
    chunk = height // terms_count
    half = height // 2

    halos = []
    for low, high in FORWARD_CUTS:
        own = operands[:, low:high]
        halos.append((shifted(own, "docs", 1), own, shifted(own, "docs", -1)))

    place = jnp.stack([docs_index, core, chip]).astype(jnp.int32)
    slab, turned = call(
        functools.partial(slab_kernel, docs_count, terms_count),
        [shape((height, 3 * depth), BF16), shape((3 * depth, height), BF16)],
        place,
        tile_rows,
        tile_cols,
        tile_count,
        tile_values,
        specs=[SMEM] * 4 + [VMEM],
        scratch=[pltpu.SMEM((height // (block // 4),), jnp.int32)],
    )
    first = (core * (terms_count // 2) + chip) * chunk
    chunk_labels = lax.dynamic_slice(labels, (first,), (chunk,))[:, None]

    parts = []
    for left, own, right in halos:
        wide = own.shape[1]
        away, kept = call(
            forward_kernel,
            [shape((half, wide), F32)] * 2,
            slab,
            left,
            own,
            right,
            flops=2 * height * 3 * depth * wide,
        )
        come = to_core(away)
        mine, ahead, across, behind = call(share_kernel, [shape((chunk, wide), F32)] * 4, kept, come)
        parts += [mine, to_chip(ahead, 1), to_chip(behind, -1), to_chip(across, 2)]
    (residual,) = call(residual_kernel, [shape((chunk, classes4), BF16)], chunk_labels, *parts)

    near = jnp.concatenate([residual, to_chip(residual, -1), to_chip(residual, 2), to_chip(residual, 1)], axis=0)
    far = to_core(near)
    to_left, to_right = call(
        send_kernel,
        [shape((depth + SCALE_ROWS, classes4), BF16)] * 2,
        turned,
        far,
        near,
        flops=2 * height * 2 * depth * classes4,
    )
    from_right = shifted(to_left, "docs", -1)
    from_left = shifted(to_right, "docs", 1)
    (own_total,) = call(
        own_kernel, [shape((depth, classes4), F32)], turned, far, near, flops=2 * height * depth * classes4
    )
    (out,) = call(total_kernel, [shape((depth, classes4), F32)], own_total, from_right, from_left)
    return out


def solution(mesh):
    in_specs = (
        P(("docs", "terms"), None, None),
        P(("docs", "terms")),
        P(("docs", "terms")),
        P(("docs", "terms")),
        P("docs"),
        P(("docs", "terms"), None),
    )
    out_specs = P(("docs", "terms"), None)
    return jax.shard_map(
        on_device, mesh=mesh, in_specs=in_specs, out_specs=out_specs, check_vma=False
    )
```

```python
import functools

import jax
import jax.numpy as jnp
from jax import lax
from jax.experimental import pallas as pl
from jax.experimental.pallas import tpu as pltpu
from jax.sharding import PartitionSpec as P

loss_weight = 4.0
F32 = jnp.float32
BF16 = jnp.bfloat16
VMEM = pl.BlockSpec(memory_space=pltpu.VMEM)
SMEM = pl.BlockSpec(memory_space=pltpu.SMEM)

SPAN = 205.0
LOWEST = 2.0**-3.75
SCALE_ROWS = 16
SMALLEST = 1e-30


def call(kernel, outs, *args, specs=None, flops=0, scratch=()):
    size = sum(o.size * o.dtype.itemsize for o in outs) + sum(a.size * a.dtype.itemsize for a in args)
    return pl.pallas_call(
        kernel,
        out_shape=outs,
        in_specs=specs or [VMEM] * len(args),
        out_specs=[VMEM] * len(outs),
        scratch_shapes=scratch,
        cost_estimate=pl.CostEstimate(flops=flops, bytes_accessed=size, transcendentals=0),
        compiler_params=pltpu.CompilerParams(vmem_limit_bytes=32 * 2**20),
    )(*args)


def shape(dims, dtype):
    return jax.ShapeDtypeStruct(dims, dtype)


def slab_kernel(docs_count, terms_count, place, rows, cols, count, tiles, slab, turned, starts):
    slots, block = tiles.shape[0], tiles.shape[1]
    docs_index, core, chip = place[0], place[1], place[2]
    height, width = slab.shape
    chunk = height // terms_count
    chips = terms_count // 2
    piece = block // 4
    row_blocks = height // block
    col_blocks = width // (3 * block)
    for part in range(height // piece):
        owner, inside = divmod(part, chunk // piece)
        owner_chip, owner_core = divmod(owner, 2)
        mine = jnp.where(core == owner_core, chips, 0)
        slot = mine + lax.rem(owner_chip - chip + chips, chips)
        starts[part] = slot * chunk + inside * piece
    slab[...] = jnp.zeros_like(slab)
    turned[...] = jnp.zeros_like(turned)

    def put(tile, carry):
        col = cols[tile]
        band = lax.rem(lax.div(col, terms_count * col_blocks) - docs_index + 1 + docs_count, docs_count)
        lane = pl.multiple_of((band * col_blocks + lax.rem(col, col_blocks)) * block, block)
        row = rows[tile] - docs_index * row_blocks
        across = pl.multiple_of(row * block, block)
        turned[pl.ds(lane, block), pl.ds(across, block)] = tiles[tile, :, :].T
        for part in range(4):
            to = pl.multiple_of(starts[row * 4 + part], piece)
            slab[pl.ds(to, piece), pl.ds(lane, block)] = tiles[tile, part * piece : (part + 1) * piece, :]
        return carry

    lax.fori_loop(0, jnp.minimum(count[0], slots), put, 0)


def forward_kernel(half_index, slab, left, own, right, out):
    depth = own.shape[0]
    half = out.shape[0]
    rows = slice(half_index * half, (half_index + 1) * half)
    total = jnp.dot(slab[rows, :depth], left[...], preferred_element_type=F32)
    total += jnp.dot(slab[rows, depth : 2 * depth], own[...], preferred_element_type=F32)
    total += jnp.dot(slab[rows, 2 * depth :], right[...], preferred_element_type=F32)
    out[...] = total


def share_kernel(kept, come, *outs):
    chunk = outs[0].shape[0]
    for i, out in enumerate(outs):
        part = slice(i * chunk, (i + 1) * chunk)
        out[...] = kept[part, :] + come[part, :]


def residual_kernel(labels, own, behind, ahead, across, out):
    combined = (own[...] + behind[...]) + (ahead[...] + across[...])
    classes = combined.shape[1] // 4
    logits = combined[:, :classes]
    shifted = jnp.exp(logits - jnp.max(logits, axis=1, keepdims=True))
    probability = shifted / jnp.sum(shifted, axis=1, keepdims=True)
    onehot = (lax.broadcasted_iota(jnp.int32, logits.shape, 1) == labels[...]).astype(F32)
    out[:, :classes] = (probability - onehot).astype(BF16)
    for j in range(1, 4):
        weighted = probability * combined[:, j * classes : (j + 1) * classes]
        curvature = weighted - probability * jnp.sum(weighted, axis=1, keepdims=True)
        out[:, j * classes : (j + 1) * classes] = curvature.astype(BF16)


def encode(values, out):
    rows = values.shape[0]
    scale = jnp.max(jnp.abs(values), axis=0, keepdims=True)
    scale = jnp.maximum(scale, SMALLEST).astype(BF16)
    out[rows:, :] = jnp.broadcast_to(scale, (SCALE_ROWS, scale.shape[1]))
    ratio = (SPAN * LOWEST) / scale.astype(F32)
    code = LOWEST + jnp.abs(values) * ratio
    for _ in range(5):
        code = code * code
    out[:rows, :] = jnp.where(values < 0, -code, code).astype(BF16)


def decode(code, scale):
    size = jnp.exp2(jnp.log2(jnp.abs(code)) * 0.03125 + 3.75) - 1.0
    size = size * (scale * (1.0 / SPAN))
    return jnp.where(code < 0, -size, size)


def product(turned, residual, band):
    depth = turned.shape[0] // 3
    return jnp.dot(turned[band * depth : (band + 1) * depth, :], residual[...], preferred_element_type=F32)


def send_kernel(band, turned, residual, out):
    encode(product(turned, residual, band), out)


def own_kernel(turned, residual, out):
    out[...] = product(turned, residual, 1)


def total_kernel(own, one, two, out):
    rows = own.shape[0]
    step = 128

    def add(i, carry):
        part = pl.ds(pl.multiple_of(i * step, step), step)
        total = own[part, :]
        for code in (one, two):
            scale = code[rows : rows + SCALE_ROWS, :].astype(F32)[0:1, :]
            total += decode(code[part, :].astype(F32), scale)
        out[part, :] = loss_weight * total
        return carry

    lax.fori_loop(0, rows // step, add, 0)


def shifted(value, axis, by):
    size = lax.axis_size(axis)
    return lax.ppermute(value, axis, [(i, (i + by) % size) for i in range(size)])


def to_chip(value, by):
    size = lax.axis_size("terms")
    return lax.ppermute(value, "terms", [(i, (i + 2 * by) % size) for i in range(size)])


def to_core(value):
    size = lax.axis_size("terms")
    return lax.ppermute(value, "terms", [(i, i ^ 1) for i in range(size)])


def on_device(tile_values, tile_rows, tile_cols, tile_count, labels, operands):
    docs_count = lax.axis_size("docs")
    terms_count = lax.axis_size("terms")
    docs_index = lax.axis_index("docs")
    terms_index = lax.axis_index("terms")
    core, chip = terms_index % 2, terms_index // 2
    block = tile_values.shape[1]
    depth, classes4 = operands.shape
    height = labels.shape[0]
    chunk = height // terms_count
    half = height // 2

    left = shifted(operands, "docs", 1)
    right = shifted(operands, "docs", -1)

    place = jnp.stack([docs_index, core, chip]).astype(jnp.int32)
    slab, turned = call(
        functools.partial(slab_kernel, docs_count, terms_count),
        [shape((height, 3 * depth), BF16), shape((3 * depth, height), BF16)],
        place,
        tile_rows,
        tile_cols,
        tile_count,
        tile_values,
        specs=[SMEM] * 4 + [VMEM],
        scratch=[pltpu.SMEM((height // (block // 4),), jnp.int32)],
    )
    chunk_labels = lax.dynamic_slice(labels, (terms_index * chunk,), (chunk,))[:, None]

    work = 2 * half * 3 * depth * classes4
    sums = [
        call(functools.partial(forward_kernel, i), [shape((half, classes4), F32)], slab, left, operands, right, flops=work)[0]
        for i in range(2)
    ]
    come = to_core(sums[0])
    mine, ahead, across, behind = call(share_kernel, [shape((chunk, classes4), F32)] * 4, sums[1], come)
    (residual,) = call(
        residual_kernel,
        [shape((chunk, classes4), BF16)],
        chunk_labels,
        mine,
        to_chip(across, 2),
        to_chip(ahead, 1),
        to_chip(behind, -1),
    )
    residual = lax.all_gather(residual, "terms", axis=0, tiled=True)

    work = 2 * height * depth * classes4
    coded = [shape((depth + SCALE_ROWS, classes4), BF16)]
    (to_left,) = call(functools.partial(send_kernel, 0), coded, turned, residual, flops=work)
    from_right = shifted(to_left, "docs", -1)
    (to_right,) = call(functools.partial(send_kernel, 2), coded, turned, residual, flops=work)
    from_left = shifted(to_right, "docs", 1)
    (own_total,) = call(own_kernel, [shape((depth, classes4), F32)], turned, residual, flops=work)
    (out,) = call(total_kernel, [shape((depth, classes4), F32)], own_total, from_right, from_left)
    return out


def solution(mesh):
    in_specs = (
        P(("docs", "terms"), None, None),
        P(("docs", "terms")),
        P(("docs", "terms")),
        P(("docs", "terms")),
        P("docs"),
        P(("docs", "terms"), None),
    )
    out_specs = P(("docs", "terms"), None)
    return jax.shard_map(
        on_device, mesh=mesh, in_specs=in_specs, out_specs=out_specs, check_vma=False
    )
```

```python
import functools

import jax
import jax.numpy as jnp
from jax import lax
from jax.experimental import pallas as pl
from jax.experimental.pallas import tpu as pltpu
from jax.sharding import PartitionSpec as P

loss_weight = 4.0
F32 = jnp.float32
BF16 = jnp.bfloat16
VMEM = pl.BlockSpec(memory_space=pltpu.VMEM)
SMEM = pl.BlockSpec(memory_space=pltpu.SMEM)

SPAN = 205.0
LOWEST = 2.0**-3.75
SCALE_ROWS = 16
SMALLEST = 1e-30


def call(kernel, outs, *args, specs=None, flops=0, scratch=()):
    size = sum(o.size * o.dtype.itemsize for o in outs) + sum(a.size * a.dtype.itemsize for a in args)
    return pl.pallas_call(
        kernel,
        out_shape=outs,
        in_specs=specs or [VMEM] * len(args),
        out_specs=[VMEM] * len(outs),
        scratch_shapes=scratch,
        cost_estimate=pl.CostEstimate(flops=flops, bytes_accessed=size, transcendentals=0),
        compiler_params=pltpu.CompilerParams(vmem_limit_bytes=16 * 2**20),
    )(*args)


def shape(dims, dtype):
    return jax.ShapeDtypeStruct(dims, dtype)


def slab_kernel(docs_count, terms_count, place, rows, cols, count, tiles, slab, turned, starts):
    slots, block = tiles.shape[0], tiles.shape[1]
    docs_index, core, chip = place[0], place[1], place[2]
    height, width = slab.shape
    chunk = height // terms_count
    chips = terms_count // 2
    piece = block // 4
    row_blocks = height // block
    col_blocks = width // (3 * block)
    for part in range(height // piece):
        owner, inside = divmod(part, chunk // piece)
        owner_chip, owner_core = divmod(owner, 2)
        mine = jnp.where(core == owner_core, chips, 0)
        slot = mine + lax.rem(owner_chip - chip + chips, chips)
        starts[part] = slot * chunk + inside * piece
    slab[...] = jnp.zeros_like(slab)
    turned[...] = jnp.zeros_like(turned)

    def put(tile, carry):
        col = cols[tile]
        band = lax.rem(lax.div(col, terms_count * col_blocks) - docs_index + 1 + docs_count, docs_count)
        lane = pl.multiple_of((band * col_blocks + lax.rem(col, col_blocks)) * block, block)
        row = rows[tile] - docs_index * row_blocks
        across = pl.multiple_of(row * block, block)
        turned[pl.ds(lane, block), pl.ds(across, block)] = tiles[tile, :, :].T
        for part in range(4):
            to = pl.multiple_of(starts[row * 4 + part], piece)
            slab[pl.ds(to, piece), pl.ds(lane, block)] = tiles[tile, part * piece : (part + 1) * piece, :]
        return carry

    lax.fori_loop(0, jnp.minimum(count[0], slots), put, 0)


def own_forward_kernel(slab, own, out):
    depth = own.shape[0]
    out[...] = jnp.dot(slab[:, depth : 2 * depth], own[...], preferred_element_type=F32)


def forward_kernel(half_index, slab, left, right, own_part, out):
    depth = left.shape[0]
    half = out.shape[0]
    rows = slice(half_index * half, (half_index + 1) * half)
    total = own_part[rows, :]
    total += jnp.dot(slab[rows, :depth], left[...], preferred_element_type=F32)
    total += jnp.dot(slab[rows, 2 * depth :], right[...], preferred_element_type=F32)
    out[...] = total


def share_kernel(kept, come, *outs):
    chunk = outs[0].shape[0]
    for i, out in enumerate(outs):
        part = slice(i * chunk, (i + 1) * chunk)
        out[...] = kept[part, :] + come[part, :]


def residual_kernel(labels, own, behind, ahead, across, out):
    combined = (own[...] + behind[...]) + (ahead[...] + across[...])
    classes = combined.shape[1] // 4
    logits = combined[:, :classes]
    shifted = jnp.exp(logits - jnp.max(logits, axis=1, keepdims=True))
    probability = shifted / jnp.sum(shifted, axis=1, keepdims=True)
    onehot = (lax.broadcasted_iota(jnp.int32, logits.shape, 1) == labels[...]).astype(F32)
    out[:, :classes] = (probability - onehot).astype(BF16)
    for j in range(1, 4):
        weighted = probability * combined[:, j * classes : (j + 1) * classes]
        curvature = weighted - probability * jnp.sum(weighted, axis=1, keepdims=True)
        out[:, j * classes : (j + 1) * classes] = curvature.astype(BF16)


def encode(values, out):
    rows = values.shape[0]
    scale = jnp.max(jnp.abs(values), axis=0, keepdims=True)
    scale = jnp.maximum(scale, SMALLEST).astype(BF16)
    out[rows:, :] = jnp.broadcast_to(scale, (SCALE_ROWS, scale.shape[1]))
    ratio = (SPAN * LOWEST) / scale.astype(F32)
    code = LOWEST + jnp.abs(values) * ratio
    for _ in range(5):
        code = code * code
    out[:rows, :] = jnp.where(values < 0, -code, code).astype(BF16)


def decode(come):
    rows = come.shape[0] - SCALE_ROWS
    code = come[:rows, :].astype(F32)
    scale = come[rows:, :].astype(F32)[0:1, :]
    size = jnp.exp2(jnp.log2(jnp.abs(code)) * 0.03125 + 3.75) - 1.0
    size = size * (scale * (1.0 / SPAN))
    return jnp.where(code < 0, -size, size)


def product(turned, residual, band):
    depth = turned.shape[0] // 3
    return jnp.dot(turned[band * depth : (band + 1) * depth, :], residual[...], preferred_element_type=F32)


def send_kernel(band, turned, residual, out):
    encode(product(turned, residual, band), out)


def own_kernel(turned, residual, out):
    out[...] = product(turned, residual, 1)


def add_kernel(own, come, out):
    out[...] = own[...] + decode(come)


def total_kernel(own, come, out):
    out[...] = loss_weight * (own[...] + decode(come))


def shifted(value, axis, by):
    size = lax.axis_size(axis)
    return lax.ppermute(value, axis, [(i, (i + by) % size) for i in range(size)])


def to_chip(value, by):
    size = lax.axis_size("terms")
    return lax.ppermute(value, "terms", [(i, (i + 2 * by) % size) for i in range(size)])


def to_core(value):
    size = lax.axis_size("terms")
    return lax.ppermute(value, "terms", [(i, i ^ 1) for i in range(size)])


def on_device(tile_values, tile_rows, tile_cols, tile_count, labels, operands):
    docs_count = lax.axis_size("docs")
    terms_count = lax.axis_size("terms")
    docs_index = lax.axis_index("docs")
    terms_index = lax.axis_index("terms")
    core, chip = terms_index % 2, terms_index // 2
    block = tile_values.shape[1]
    depth, classes4 = operands.shape
    height = labels.shape[0]
    chunk = height // terms_count
    half = height // 2

    left = shifted(operands, "docs", 1)
    right = shifted(operands, "docs", -1)

    place = jnp.stack([docs_index, core, chip]).astype(jnp.int32)
    slab, turned = call(
        functools.partial(slab_kernel, docs_count, terms_count),
        [shape((height, 3 * depth), BF16), shape((3 * depth, height), BF16)],
        place,
        tile_rows,
        tile_cols,
        tile_count,
        tile_values,
        specs=[SMEM] * 4 + [VMEM],
        scratch=[pltpu.SMEM((height // (block // 4),), jnp.int32)],
    )
    chunk_labels = lax.dynamic_slice(labels, (terms_index * chunk,), (chunk,))[:, None]

    (own_part,) = call(
        own_forward_kernel,
        [shape((height, classes4), F32)],
        slab,
        operands,
        flops=2 * height * depth * classes4,
    )
    work = 2 * half * 2 * depth * classes4
    sums = [
        call(
            functools.partial(forward_kernel, i),
            [shape((half, classes4), F32)],
            slab,
            left,
            right,
            own_part,
            flops=work,
        )[0]
        for i in range(2)
    ]
    come = to_core(sums[0])
    mine, ahead, across, behind = call(share_kernel, [shape((chunk, classes4), F32)] * 4, sums[1], come)
    (residual,) = call(
        residual_kernel,
        [shape((chunk, classes4), BF16)],
        chunk_labels,
        mine,
        to_chip(across, 2),
        to_chip(ahead, 1),
        to_chip(behind, -1),
    )
    residual = lax.all_gather(residual, "terms", axis=0, tiled=True)

    work = 2 * height * depth * classes4
    coded = [shape((depth + SCALE_ROWS, classes4), BF16)]
    (to_right,) = call(functools.partial(send_kernel, 2), coded, turned, residual, flops=work)
    from_left = shifted(to_right, "docs", 1)
    (to_left,) = call(functools.partial(send_kernel, 0), coded, turned, residual, flops=work)
    from_right = shifted(to_left, "docs", -1)
    (total,) = call(own_kernel, [shape((depth, classes4), F32)], turned, residual, flops=work)
    (total,) = call(add_kernel, [shape((depth, classes4), F32)], total, from_left)
    (out,) = call(total_kernel, [shape((depth, classes4), F32)], total, from_right)
    return out


def solution(mesh):
    in_specs = (
        P(("docs", "terms"), None, None),
        P(("docs", "terms")),
        P(("docs", "terms")),
        P(("docs", "terms")),
        P("docs"),
        P(("docs", "terms"), None),
    )
    out_specs = P(("docs", "terms"), None)
    return jax.shard_map(
        on_device, mesh=mesh, in_specs=in_specs, out_specs=out_specs, check_vma=False
    )
```

```python
import functools

import jax
import jax.numpy as jnp
from jax import lax
from jax.experimental import pallas as pl
from jax.experimental.pallas import tpu as pltpu
from jax.sharding import PartitionSpec as P

loss_weight = 4.0
F32 = jnp.float32
BF16 = jnp.bfloat16
VMEM = pl.BlockSpec(memory_space=pltpu.VMEM)
SMEM = pl.BlockSpec(memory_space=pltpu.SMEM)

SPAN = 205.0
LOWEST = 2.0**-3.75
SCALE_ROWS = 16
SMALLEST = 1e-30


def call(kernel, outs, *args, specs=None, out_spec=VMEM, flops=0, scratch=()):
    size = sum(o.size * o.dtype.itemsize for o in outs) + sum(a.size * a.dtype.itemsize for a in args)
    return pl.pallas_call(
        kernel,
        out_shape=outs,
        in_specs=specs or [VMEM] * len(args),
        out_specs=[out_spec] * len(outs),
        scratch_shapes=scratch,
        cost_estimate=pl.CostEstimate(flops=flops, bytes_accessed=size, transcendentals=0),
        compiler_params=pltpu.CompilerParams(vmem_limit_bytes=16 * 2**20),
    )(*args)


def shape(dims, dtype):
    return jax.ShapeDtypeStruct(dims, dtype)


def slab_kernel(docs_count, terms_count, place, rows, cols, count, tiles, slab, turned, starts):
    slots, block = tiles.shape[0], tiles.shape[1]
    docs_index, core, chip = place[0], place[1], place[2]
    height, width = slab.shape
    chunk = height // terms_count
    chips = terms_count // 2
    piece = block // 4
    row_blocks = height // block
    col_blocks = width // (3 * block)
    for part in range(height // piece):
        owner, inside = divmod(part, chunk // piece)
        owner_chip, owner_core = divmod(owner, 2)
        mine = jnp.where(core == owner_core, chips, 0)
        slot = mine + lax.rem(owner_chip - chip + chips, chips)
        starts[part] = slot * chunk + inside * piece
    slab[...] = jnp.zeros_like(slab)
    turned[...] = jnp.zeros_like(turned)

    def put(tile, carry):
        col = cols[tile]
        band = lax.rem(lax.div(col, terms_count * col_blocks) - docs_index + 1 + docs_count, docs_count)
        lane = pl.multiple_of((band * col_blocks + lax.rem(col, col_blocks)) * block, block)
        row = rows[tile] - docs_index * row_blocks
        across = pl.multiple_of(row * block, block)
        turned[pl.ds(lane, block), pl.ds(across, block)] = tiles[tile, :, :].T
        for part in range(4):
            to = pl.multiple_of(starts[row * 4 + part], piece)
            slab[pl.ds(to, piece), pl.ds(lane, block)] = tiles[tile, part * piece : (part + 1) * piece, :]
        return carry

    lax.fori_loop(0, jnp.minimum(count[0], slots), put, 0)


def own_forward_kernel(slab, own, out):
    depth = own.shape[0]
    out[...] = jnp.dot(slab[:, depth : 2 * depth], own[...], preferred_element_type=F32)


def forward_kernel(half_index, slab, left, right, own_part, out):
    depth = left.shape[0]
    half = out.shape[0]
    rows = slice(half_index * half, (half_index + 1) * half)
    total = own_part[rows, :]
    total += jnp.dot(slab[rows, :depth], left[...], preferred_element_type=F32)
    total += jnp.dot(slab[rows, 2 * depth :], right[...], preferred_element_type=F32)
    out[...] = total


def share_kernel(places, kept, come, *outs):
    chunk = outs[0].shape[0]
    for place, out in zip(places, outs):
        part = slice(place * chunk, (place + 1) * chunk)
        out[...] = kept[part, :] + come[part, :]


def residual_kernel(labels, own, behind, ahead, across, out):
    combined = (own[...] + behind[...]) + (ahead[...] + across[...])
    classes = combined.shape[1] // 4
    logits = combined[:, :classes]
    shifted = jnp.exp(logits - jnp.max(logits, axis=1, keepdims=True))
    probability = shifted / jnp.sum(shifted, axis=1, keepdims=True)
    onehot = (lax.broadcasted_iota(jnp.int32, logits.shape, 1) == labels[...]).astype(F32)
    out[:, :classes] = (probability - onehot).astype(BF16)
    for j in range(1, 4):
        weighted = probability * combined[:, j * classes : (j + 1) * classes]
        curvature = weighted - probability * jnp.sum(weighted, axis=1, keepdims=True)
        out[:, j * classes : (j + 1) * classes] = curvature.astype(BF16)


def encode(values, out, cut):
    rows = values.shape[0]
    scale = jnp.max(jnp.abs(values), axis=0, keepdims=True)
    scale = jnp.maximum(scale, SMALLEST).astype(BF16)
    out[rows:, cut] = jnp.broadcast_to(scale, (SCALE_ROWS, scale.shape[1]))
    ratio = (SPAN * LOWEST) / scale.astype(F32)
    code = LOWEST + jnp.abs(values) * ratio
    for _ in range(5):
        code = code * code
    out[:rows, cut] = jnp.where(values < 0, -code, code).astype(BF16)


def decode(come, part):
    rows = come.shape[0] - SCALE_ROWS
    code = come[part, :].astype(F32)
    scale = come[rows:, :].astype(F32)[0:1, :]
    size = jnp.exp2(jnp.log2(jnp.abs(code)) * 0.03125 + 3.75) - 1.0
    size = size * (scale * (1.0 / SPAN))
    return jnp.where(code < 0, -size, size)


def product(turned, residual, band, cut):
    depth = turned.shape[0] // 3
    return jnp.dot(turned[band * depth : (band + 1) * depth, :], residual[:, cut], preferred_element_type=F32)


def send_kernel(band, turned, residual, out):
    wide = residual.shape[1] // 2
    for low in (0, wide):
        cut = slice(low, low + wide)
        encode(product(turned, residual, band, cut), out, cut)


def own_kernel(turned, residual, out):
    out[...] = product(turned, residual, 1, slice(0, residual.shape[1]))


def add_kernel(own, come, out):
    out[...] = own[...] + decode(come, slice(0, own.shape[0]))


def total_kernel(own, come, out, whole, sems):
    count = sems.shape[0]
    step = own.shape[0] // count
    copies = []
    for i in range(count):
        part = slice(i * step, (i + 1) * step)
        whole[part, :] = loss_weight * (own[part, :] + decode(come, part))
        copies.append(pltpu.make_async_copy(whole.at[part, :], out.at[part, :], sems.at[i]))
        copies[-1].start()
    for copy in copies:
        copy.wait()


def shifted(value, axis, by):
    size = lax.axis_size(axis)
    return lax.ppermute(value, axis, [(i, (i + by) % size) for i in range(size)])


def to_chip(value, by):
    size = lax.axis_size("terms")
    return lax.ppermute(value, "terms", [(i, (i + 2 * by) % size) for i in range(size)])


def to_core(value):
    size = lax.axis_size("terms")
    return lax.ppermute(value, "terms", [(i, i ^ 1) for i in range(size)])


def on_device(tile_values, tile_rows, tile_cols, tile_count, labels, operands):
    docs_count = lax.axis_size("docs")
    terms_count = lax.axis_size("terms")
    docs_index = lax.axis_index("docs")
    terms_index = lax.axis_index("terms")
    core, chip = terms_index % 2, terms_index // 2
    block = tile_values.shape[1]
    depth, classes4 = operands.shape
    height = labels.shape[0]
    chunk = height // terms_count
    half = height // 2

    left = shifted(operands, "docs", 1)
    right = shifted(operands, "docs", -1)

    place = jnp.stack([docs_index, core, chip]).astype(jnp.int32)
    slab, turned = call(
        functools.partial(slab_kernel, docs_count, terms_count),
        [shape((height, 3 * depth), BF16), shape((3 * depth, height), BF16)],
        place,
        tile_rows,
        tile_cols,
        tile_count,
        tile_values,
        specs=[SMEM] * 4 + [VMEM],
        scratch=[pltpu.SMEM((height // (block // 4),), jnp.int32)],
    )
    chunk_labels = lax.dynamic_slice(labels, (terms_index * chunk,), (chunk,))[:, None]

    (own_part,) = call(
        own_forward_kernel,
        [shape((height, classes4), F32)],
        slab,
        operands,
        flops=2 * height * depth * classes4,
    )
    work = 2 * half * 2 * depth * classes4
    sums = [
        call(
            functools.partial(forward_kernel, i),
            [shape((half, classes4), F32)],
            slab,
            left,
            right,
            own_part,
            flops=work,
        )[0]
        for i in range(2)
    ]
    come = to_core(sums[0])
    small = shape((chunk, classes4), F32)
    (across,) = call(functools.partial(share_kernel, (2,)), [small], sums[1], come)
    across = to_chip(across, 2)
    mine, ahead, behind = call(functools.partial(share_kernel, (0, 1, 3)), [small] * 3, sums[1], come)
    (residual,) = call(
        residual_kernel,
        [shape((chunk, classes4), BF16)],
        chunk_labels,
        mine,
        across,
        to_chip(ahead, 1),
        to_chip(behind, -1),
    )
    residual = lax.all_gather(residual, "terms", axis=0, tiled=True)

    work = 2 * height * depth * classes4
    coded = [shape((depth + SCALE_ROWS, classes4), BF16)]
    (to_right,) = call(functools.partial(send_kernel, 2), coded, turned, residual, flops=work)
    from_left = shifted(to_right, "docs", 1)
    (to_left,) = call(functools.partial(send_kernel, 0), coded, turned, residual, flops=work)
    from_right = shifted(to_left, "docs", -1)
    (total,) = call(own_kernel, [shape((depth, classes4), F32)], turned, residual, flops=work)
    (total,) = call(add_kernel, [shape((depth, classes4), F32)], total, from_left)
    (out,) = call(
        total_kernel,
        [shape((depth, classes4), F32)],
        total,
        from_right,
        out_spec=pl.BlockSpec(memory_space=pl.ANY),
        scratch=[pltpu.VMEM((depth, classes4), F32), pltpu.SemaphoreType.DMA((4,))],
    )
    return out


def solution(mesh):
    in_specs = (
        P(("docs", "terms"), None, None),
        P(("docs", "terms")),
        P(("docs", "terms")),
        P(("docs", "terms")),
        P("docs"),
        P(("docs", "terms"), None),
    )
    out_specs = P(("docs", "terms"), None)
    return jax.shard_map(
        on_device, mesh=mesh, in_specs=in_specs, out_specs=out_specs, check_vma=False
    )
```
